128 devices in a mesh: sample: 8 (over x_lo, z), head: 16 (over x_hi, y, core).
Axes of the slice: x: 4 (x_hi: 2, x_lo: 2; x = x_hi * 2 + x_lo), y: 4, z: 4, core: 2. Of those that a mesh axis runs over, the one named last changes fastest.
Arguments:
- queries: bfloat16 [8, 2048, 8192], P('sample', 'head'), may hold values from -200 to 200
- image_tokens: bfloat16 [8, 1664, 7680], P('sample', None, 'head'), may hold values from -6 to 6
- kv_weight: bfloat16 [7680, 8, 2, 128], P('head', 'sample'), may hold values from -0.0625 to 0.0625
- attn_gate: float32 [1], replicated, may hold values from 0.3 to 1.5
- image_counts: int32 [8], P('sample'), may hold values from 832 to 1664, as said below
- response_lengths: int32 [8], P('sample'), may hold values from 512 to 2048, as said below
Outputs:
- gated: bfloat16 [8, 2048, 8192], P('sample', 'head')
The draws below stay inside these ranges and needn't reach their ends.
Inputs may be any that keep to these rules, and one draw needn't show every extreme that they name: `image_counts`: in every draw at least one sample has all 1664 slots filled. `response_lengths`: in every draw at least one sample has all 2048 tokens.
All inputs are finite; a program needn't handle non-finite values.
Results may differ from the reference program's by a relative error of at most 0.01.
Values may be sent and summed in bfloat16 or wider, within the bound.
No kernel may reach another device: no remote copies, remote signals or barrier semaphores. Data moves between devices by JAX's collectives and lax.ppermute only.
A program may use at most 128 MiB of HBM per device.

```python
import jax
import jax.numpy as jnp
from jax import lax

QH = 64
KVH = 8
HD = 128
IMG_D = 7680
IMG = 1664
LEN = 2048
SAMPLES = 8
N_HEAD = 16


def draw_queries(key, part):
    key = jax.random.fold_in(key, 11)
    key_base = jax.random.fold_in(key, 0)
    shape = (SAMPLES, LEN, QH * HD)
    values = jnp.clip(jax.random.normal(key_base, shape, jnp.float32) * 2.5, -15.0, 15.0)
    return jnp.clip(values, -200.0, 200.0).astype(jnp.bfloat16)


def draw_image_counts(key, part):
    key = jax.random.fold_in(key, 23)
    key_values, key_full = jax.random.split(key)
    values = jax.random.randint(key_values, (SAMPLES,), IMG // 2, IMG + 1)
    fullest = jax.random.randint(key_full, (), 0, SAMPLES)
    return jnp.where(jnp.arange(SAMPLES) == fullest, IMG, values).astype(jnp.int32)


def draw_response_lengths(key, part):
    key = jax.random.fold_in(key, 37)
    key_values, key_full = jax.random.split(key)
    values = jax.random.randint(key_values, (SAMPLES,), LEN // 4, LEN + 1)
    fullest = jax.random.randint(key_full, (), 0, SAMPLES)
    return jnp.where(jnp.arange(SAMPLES) == fullest, LEN, values).astype(jnp.int32)


def level_of(key, shape, cuts, smallest, high):
    def one(axis_at, blocks):
        heights = jax.random.uniform(jax.random.fold_in(jax.random.fold_in(key, 6), axis_at), (blocks,), jnp.float32, smallest / len(cuts), high / len(cuts))
        return jnp.repeat(jnp.exp(heights), shape[axis_at] // blocks).reshape((-1,) + (1,) * (len(shape) - axis_at - 1))

    gain = one(*cuts[0])
    for cut in cuts[1:]:
        gain = gain * one(*cut)
    return gain


def bell_draw(own_key, shape, spread, reach, pieces=(), held_as=jnp.bfloat16):
    gain = level_of(own_key, shape, pieces, -0.22, 0.18) if pieces else 1.0
    array = jax.random.normal(own_key, shape, jnp.float32) * spread * gain
    return jnp.minimum(jnp.maximum(array, -reach), reach).astype(held_as)


def setup_inputs(seed: int = 0) -> dict:
    key_of = jax.random.split(jax.random.key(seed), 7)
    queries = draw_queries(jax.random.fold_in(key_of[6], 71), 0)
    image_tokens = bell_draw(key_of[1], (SAMPLES, IMG, IMG_D), 1.0, 6.0, ((0, 8), (2, 16)))
    kv_weight = bell_draw(key_of[2], (IMG_D, KVH, 2, HD), IMG_D ** -0.5, 0.0625, ((0, 16), (1, 8)))
    attn_gate = jnp.clip(jax.random.uniform(key_of[3], (1,), jnp.float32, 0.3, 1.5), 0.3, 1.5)
    image_counts = draw_image_counts(jax.random.fold_in(key_of[6], 71), 0)
    response_lengths = draw_response_lengths(jax.random.fold_in(key_of[6], 71), 0)
    return {"queries": queries, "image_tokens": image_tokens, "kv_weight": kv_weight, "attn_gate": attn_gate, "image_counts": image_counts, "response_lengths": response_lengths}


def attend(query_rows, key_cols, value_cols, keep_keys):
    total_rows = query_rows.shape[0]
    head_size = query_rows.shape[1]
    block_size = 1024 if total_rows % 1024 == 0 else total_rows
    scale_factor = head_size ** -0.5

    def one_block(block_rows):
        scores = jnp.dot(block_rows, key_cols, preferred_element_type=jnp.float32) * scale_factor
        scores = jnp.where(keep_keys[None, :], scores, -1e30)
        top_score = jnp.max(scores, axis=1, keepdims=True)
        exponent = jnp.exp(scores - top_score)
        denominator = jnp.sum(exponent, axis=1, keepdims=True)
        weights = exponent.astype(jnp.bfloat16)
        mixed_rows = lax.dot_general(weights, value_cols, (((1,), (1,)), ((), ())), preferred_element_type=jnp.float32)
        return mixed_rows / denominator

    blocked = query_rows.reshape(total_rows // block_size, block_size, head_size)
    return lax.map(one_block, blocked).reshape(total_rows, head_size)


def reference(queries, image_tokens, kv_weight, attn_gate, image_counts, response_lengths):
    part_width = IMG_D // N_HEAD
    group_size = QH // KVH
    flat_weight = kv_weight.reshape(N_HEAD, part_width, KVH * 2 * HD)
    gate_value = jnp.tanh(attn_gate[0])

    def one_sample(sample_index):
        image_now = lax.dynamic_index_in_dim(image_tokens, sample_index, 0, keepdims=False)
        image_parts = image_now.reshape(IMG, N_HEAD, part_width)

        def add_part(running, part_index):
            image_part = lax.dynamic_index_in_dim(image_parts, part_index, 1, keepdims=False)
            weight_part = lax.dynamic_index_in_dim(flat_weight, part_index, 0, keepdims=False)
            part_term = jnp.dot(image_part, weight_part, preferred_element_type=jnp.float32)
            return running + part_term, None

        summed, _ = lax.scan(add_part, jnp.zeros((IMG, KVH * 2 * HD), jnp.float32), jnp.arange(N_HEAD, dtype=jnp.int32))
        kv_all = summed.astype(jnp.bfloat16).reshape(IMG, KVH, 2, HD)
        keep_keys = jnp.arange(IMG, dtype=jnp.int32) < lax.dynamic_index_in_dim(image_counts, sample_index, 0, keepdims=False)
        query_all = lax.dynamic_index_in_dim(queries, sample_index, 0, keepdims=False).reshape(LEN, KVH, group_size * HD)

        def one_group(group_index):
            key_cols = lax.dynamic_index_in_dim(kv_all[:, :, 0, :], group_index, 1, keepdims=False).T
            value_cols = lax.dynamic_index_in_dim(kv_all[:, :, 1, :], group_index, 1, keepdims=False).T
            query_rows = lax.dynamic_index_in_dim(query_all, group_index, 1, keepdims=False).reshape(LEN * group_size, HD)
            return attend(query_rows, key_cols, value_cols, keep_keys).astype(jnp.bfloat16).reshape(LEN, group_size * HD)

        per_group = lax.map(one_group, jnp.arange(KVH, dtype=jnp.int32))
        attention = per_group.transpose(1, 0, 2).reshape(LEN, QH * HD)
        live_rows = jnp.arange(LEN, dtype=jnp.int32) < lax.dynamic_index_in_dim(response_lengths, sample_index, 0, keepdims=False)
        gated_rows = jnp.where(live_rows[:, None], gate_value * attention.astype(jnp.float32), 0.0)
        return gated_rows.astype(jnp.bfloat16)

    return lax.map(one_sample, jnp.arange(SAMPLES, dtype=jnp.int32))
```

```python
import functools

import jax
import jax.numpy as jnp
from jax import lax
from jax.experimental import pallas as pl
from jax.experimental.pallas import tpu as pltpu
from jax.sharding import Mesh
from jax.sharding import PartitionSpec as P

XL, Z, XH, Y, C = "xl", "z", "xh", "y", "c"
CHIPS = (XH, Y)
N_CHIPS = 8
VMEM_LIMIT = 48 * 1024 * 1024


def params():
    return pltpu.CompilerParams(vmem_limit_bytes=VMEM_LIMIT)


def weight_round(flip):
    pairs = []
    for xl in range(2):
        for z in range(4):
            for b in range(2):
                pairs.append(((xl * 4 + z) * 2 + b, ((b ^ flip) * 4 + z) * 2 + xl))
    return pairs


def ring(size, step):
    return [(i, (i + step) % size) for i in range(size)]


def project_kernel(n_heads, *refs):
    w_refs, (own_ref, other_ref), out_ref = refs[:n_heads], refs[n_heads : n_heads + 2], refs[-1]
    for h in range(n_heads):
        acc = jnp.dot(w_refs[h][0], own_ref[...], preferred_element_type=jnp.float32)
        acc += jnp.dot(w_refs[h][1], other_ref[...], preferred_element_type=jnp.float32)
        out_ref[:, h] = acc.astype(jnp.bfloat16).reshape(out_ref.shape[0], out_ref.shape[2], out_ref.shape[3])


def project(weights, own_image, other_image):
    n_heads = len(weights)
    rows = weights[0].shape[1] // N_CHIPS
    tokens = own_image.shape[1]
    flops = 2 * n_heads * weights[0].shape[1] * tokens * own_image.shape[0] * 2
    return pl.pallas_call(
        functools.partial(project_kernel, n_heads),
        out_shape=jax.ShapeDtypeStruct((N_CHIPS, n_heads, rows, tokens), jnp.bfloat16),
        compiler_params=params(),
        cost_estimate=pl.CostEstimate(flops=flops, bytes_accessed=6 << 20, transcendentals=0),
        name="project",
    )(*weights, own_image, other_image)


def sum_kernel(info_ref, parts_ref, out_ref):
    total = parts_ref[0].astype(jnp.float32)
    for d in range(1, N_CHIPS):
        total += parts_ref[d].astype(jnp.float32)
    first = jnp.where(info_ref[1] == 1, total[..., :1], 0.0)
    slot = lax.broadcasted_iota(jnp.int32, total.shape, 2)
    total = jnp.where(slot < info_ref[0], total, first).astype(jnp.bfloat16)
    for d in range(N_CHIPS):
        out_ref[d] = total


def sum_parts(info, parts):
    return pl.pallas_call(
        sum_kernel,
        out_shape=jax.ShapeDtypeStruct(parts.shape, jnp.bfloat16),
        in_specs=[pl.BlockSpec(memory_space=pltpu.SMEM), pl.BlockSpec(memory_space=pltpu.VMEM)],
        compiler_params=params(),
        cost_estimate=pl.CostEstimate(flops=1 << 20, bytes_accessed=4 << 20, transcendentals=0),
        name="sum_parts",
    )(info, parts)


def attend_kernel(head_dim, scalars, gate_ref, kv_ref, q_own, q_other, held, out_own, out_other):
    del held
    rows = q_own.shape[0]
    tokens = kv_ref.shape[2]
    keys = kv_ref[:4].reshape(head_dim, tokens)
    slot = lax.broadcasted_iota(jnp.int32, (head_dim, tokens), 1)
    row = lax.broadcasted_iota(jnp.int32, (head_dim, tokens), 0)
    counted = ((slot < scalars[2]) & (row == 0)).astype(jnp.float32).astype(jnp.bfloat16)
    values = jnp.concatenate([kv_ref[4:].reshape(head_dim, tokens), counted], axis=0)
    gate = gate_ref[0]
    log2e = 1.4426950408889634
    factor = head_dim**-0.5 * log2e
    live = []
    for first in (scalars[3], scalars[4]):
        live.append(first + lax.broadcasted_iota(jnp.int32, (rows, head_dim), 0) < scalars[5])
    live = jnp.concatenate(live, axis=0)
    for h in range(q_own.shape[1] // head_dim):
        cols = slice(h * head_dim, (h + 1) * head_dim)
        q = jnp.concatenate([q_own[:, cols], q_other[:, cols]], axis=0)
        scores = jnp.dot(q, keys, preferred_element_type=jnp.float32)
        top = jnp.max(scores, axis=1, keepdims=True) * factor
        weights = jnp.exp2(scores * factor - top).astype(jnp.bfloat16)
        mixed = lax.dot_general(weights, values, (((1,), (1,)), ((), ())), preferred_element_type=jnp.float32)
        attention = (mixed[:, :head_dim] / mixed[:, head_dim : head_dim + 1]).astype(jnp.bfloat16)
        gated = jnp.where(live, gate * attention.astype(jnp.float32), 0.0).astype(jnp.bfloat16)
        out_own[:, cols] = gated[:rows]
        out_other[:, cols] = gated[rows:]


def attend(scalars, gate, kv, head, q_own, q_other, held, head_dim):
    rows = q_own.shape[0]
    width = q_other.shape[1] // 4
    tokens = kv.shape[-1]
    n_heads = kv.shape[1]
    aliases = {} if held is None else {6: 0}
    if held is None:
        held = jnp.zeros((8, 128), jnp.bfloat16)
    grid_spec = pltpu.PrefetchScalarGridSpec(
        num_scalar_prefetch=1,
        grid=(1,),
        in_specs=[
            pl.BlockSpec(memory_space=pltpu.SMEM),
            pl.BlockSpec((N_CHIPS, pl.Squeezed(), kv.shape[2], tokens), lambda i, s: (0, head, 0, 0)),
            pl.BlockSpec((rows, width), lambda i, s: (0, s[0])),
            pl.BlockSpec((rows, width), lambda i, s: (0, s[1])),
            pl.BlockSpec(memory_space=pl.ANY),
        ],
        out_specs=[
            pl.BlockSpec((rows, width), lambda i, s: (0, s[0])),
            pl.BlockSpec((rows, width), lambda i, s: (0, 0)),
        ],
    )
    n_q = 2 * rows * width // head_dim
    return pl.pallas_call(
        functools.partial(attend_kernel, head_dim),
        out_shape=[
            jax.ShapeDtypeStruct(q_own.shape, jnp.bfloat16),
            jax.ShapeDtypeStruct((rows, width), jnp.bfloat16),
        ],
        grid_spec=grid_spec,
        input_output_aliases=({5: 0} if aliases else {}),
        compiler_params=params(),
        cost_estimate=pl.CostEstimate(
            flops=4 * n_q * tokens * head_dim * 2, bytes_accessed=4 << 20, transcendentals=n_q * tokens
        ),
        name="attend",
    )(scalars, gate, kv, q_own, q_other, held)


def place_kernel(scalars, received, held, out):
    del held
    out[...] = received[...]


def place(scalars, received, held):
    rows, width = received.shape
    return pl.pallas_call(
        place_kernel,
        out_shape=jax.ShapeDtypeStruct(held.shape, held.dtype),
        grid_spec=pltpu.PrefetchScalarGridSpec(
            num_scalar_prefetch=1,
            grid=(1,),
            in_specs=[
                pl.BlockSpec((rows, width), lambda i, s: (0, 0)),
                pl.BlockSpec(memory_space=pl.ANY),
            ],
            out_specs=pl.BlockSpec((rows, width), lambda i, s: (0, s[6])),
        ),
        input_output_aliases={2: 0},
        compiler_params=params(),
        name="place",
    )(scalars, received, held)


def on_device(queries, image_tokens, kv_weight, attn_gate, image_counts, response_lengths):
    rows = queries.shape[1]
    head_dim = kv_weight.shape[3]
    half = queries.shape[2] // 2
    xl, z, xh, y, c = (lax.axis_index(a) for a in (XL, Z, XH, Y, C))
    q = queries[0]
    image = image_tokens[0].T
    w_own = kv_weight[:, 0].transpose(1, 2, 0).reshape(2 * head_dim, -1)

    firsts = [lax.ppermute(w_own, (XL, Z, C), weight_round(flip)) for flip in range(2)]
    swapped = (xl ^ c) == 1
    stack = jnp.stack([jnp.where(swapped, firsts[1], firsts[0]), jnp.where(swapped, firsts[0], firsts[1])])
    image_other = lax.ppermute(image, C, ring(2, 1))
    w_next = lax.ppermute(stack, Z, ring(4, -1))
    w_prev = lax.ppermute(stack, Z, ring(4, 1))
    w_far = lax.ppermute(stack, Z, ring(4, 2))
    q_give = lax.dynamic_slice_in_dim(q, (1 - c) * half, half, axis=1)
    q_other = lax.ppermute(q_give, C, ring(2, 1))

    chip = xh * 4 + y
    count = image_counts[0]
    sum_info = jnp.stack([count, (chip < 4).astype(jnp.int32)])
    gate = jnp.tanh(attn_gate)
    mine = (chip * 2 + c) * rows
    theirs = (chip * 2 + 1 - c) * rows

    out = None
    pending = []
    chunks = [([stack], [0]), ([w_next, w_prev], [1, 3]), ([w_far], [2])]
    gathered = []
    for weights, steps in chunks:
        parts = project(weights, image, image_other)
        n_heads, part_rows, tokens = parts.shape[1:]
        flat = (N_CHIPS, n_heads * part_rows, tokens)
        parts = lax.all_to_all(parts.reshape(flat), CHIPS, 0, 0, tiled=True)
        summed = sum_parts(sum_info, parts.reshape(N_CHIPS, n_heads, part_rows, tokens))
        kv = lax.all_to_all(summed.reshape(flat), CHIPS, 0, 0, tiled=True)
        gathered.append(kv.reshape(N_CHIPS, n_heads, part_rows, tokens))
    for (weights, steps), kv in zip(chunks, gathered):
        for i, step in enumerate(steps):
            head = (z + step) % 4
            scalars = jnp.stack(
                [c * 4 + head, head, count, mine, theirs, response_lengths[0], (1 - c) * 4 + head]
            ).astype(jnp.int32)
            out, give = attend(scalars, gate, kv, i, q, q_other, out, head_dim)
            pending.append((scalars, lax.ppermute(give, C, ring(2, 1))))
    for scalars, received in pending:
        out = place(scalars, received, out)
    return out[None]


def solution(mesh):
    fine = Mesh(mesh.devices.reshape(2, 4, 2, 4, 2), (XL, Z, XH, Y, C))
    sample, head = (XL, Z), (XH, Y, C)
    placed = (
        P(sample, head, None),
        P(sample, None, head),
        P(head, sample, None, None),
        P(),
        P(sample),
        P(sample),
    )
    return jax.shard_map(
        on_device, mesh=fine, in_specs=placed, out_specs=P(sample, head, None), check_vma=False
    )
```

```python
import functools

import jax
import jax.numpy as jnp
from jax import lax
from jax.experimental import pallas as pl
from jax.experimental.pallas import tpu as pltpu
from jax.sharding import Mesh
from jax.sharding import PartitionSpec as P

XL, Z, XH, Y, C = "xl", "z", "xh", "y", "c"
CHIPS = (XH, Y)
N_CHIPS = 8
MIB = 1024 * 1024


def params(mib):
    return pltpu.CompilerParams(vmem_limit_bytes=mib * MIB)


def weight_round(flip):
    pairs = []
    for xl in range(2):
        for z in range(4):
            for b in range(2):
                pairs.append(((xl * 4 + z) * 2 + b, ((b ^ flip) * 4 + z) * 2 + xl))
    return pairs


def ring(size, step):
    return [(i, (i + step) % size) for i in range(size)]


def project_kernel(w_ref, own_ref, other_ref, held, out_ref):
    del held
    acc = jnp.dot(w_ref[0], own_ref[...], preferred_element_type=jnp.float32)
    acc += jnp.dot(w_ref[1], other_ref[...], preferred_element_type=jnp.float32)
    out_ref[...] = acc.astype(jnp.bfloat16).reshape(out_ref.shape)


def project(weight, own_image, other_image, side, held):
    kv_rows = weight.shape[1]
    tokens = own_image.shape[1]
    groups = N_CHIPS // 2
    shape = (N_CHIPS, kv_rows // groups, tokens)
    whole = pl.BlockSpec(memory_space=pltpu.VMEM)
    return pl.pallas_call(
        project_kernel,
        out_shape=jax.ShapeDtypeStruct(shape, jnp.bfloat16),
        grid=(1,),
        in_specs=[whole, whole, whole, pl.BlockSpec(memory_space=pl.ANY)],
        out_specs=pl.BlockSpec((groups,) + shape[1:], lambda i: (side, 0, 0)),
        input_output_aliases={3: 0} if held.shape == shape else {},
        compiler_params=params(20),
        cost_estimate=pl.CostEstimate(
            flops=2 * kv_rows * tokens * own_image.shape[0] * 2, bytes_accessed=5 * MIB, transcendentals=0
        ),
        name="project",
    )(weight, own_image, other_image, held)


def sum_kernel(info_ref, parts_ref, out_ref):
    total = parts_ref[0].astype(jnp.float32)
    for d in range(1, N_CHIPS):
        total += parts_ref[d].astype(jnp.float32)
    first = jnp.where(info_ref[1] == 1, total[:, :1], 0.0)
    slot = lax.broadcasted_iota(jnp.int32, total.shape, 1)
    total = jnp.where(slot < info_ref[0], total, first).astype(jnp.bfloat16)
    for d in range(out_ref.shape[0]):
        out_ref[d] = total


def sum_parts(info, parts):
    return pl.pallas_call(
        sum_kernel,
        out_shape=jax.ShapeDtypeStruct((parts.shape[0] // 2,) + parts.shape[1:], jnp.bfloat16),
        in_specs=[pl.BlockSpec(memory_space=pltpu.SMEM), pl.BlockSpec(memory_space=pltpu.VMEM)],
        compiler_params=params(16),
        cost_estimate=pl.CostEstimate(flops=1 << 20, bytes_accessed=4 << 20, transcendentals=0),
        name="sum_parts",
    )(info, parts)


def attend_kernel(head_dim, scalars, gate_ref, kv_ref, q_0, q_1, held, out_0, out_1):
    del held
    rows = q_0.shape[0]
    tokens = kv_ref.shape[2]
    keys = kv_ref[:2].reshape(head_dim, tokens)
    slot = lax.broadcasted_iota(jnp.int32, (head_dim, tokens), 1)
    row = lax.broadcasted_iota(jnp.int32, (head_dim, tokens), 0)
    counted = ((slot < scalars[1]) & (row == 0)).astype(jnp.float32).astype(jnp.bfloat16)
    values = jnp.concatenate([kv_ref[2:].reshape(head_dim, tokens), counted], axis=0)
    gate = gate_ref[0]
    factor = head_dim**-0.5 * 1.4426950408889634
    live = []
    for first in (scalars[2], scalars[3]):
        live.append(first + lax.broadcasted_iota(jnp.int32, (rows, head_dim), 0) < scalars[4])
    live = jnp.concatenate(live + live, axis=0)
    for h in range(0, q_0.shape[1] // head_dim, 2):
        cols = [slice(k * head_dim, (k + 1) * head_dim) for k in (h, h + 1)]
        q = jnp.concatenate([ref[:, k] for k in cols for ref in (q_0, q_1)], axis=0)
        scores = jnp.dot(q, keys, preferred_element_type=jnp.float32)
        top = jnp.max(scores, axis=1, keepdims=True) * factor
        weights = jnp.exp2(scores * factor - top).astype(jnp.bfloat16)
        mixed = lax.dot_general(weights, values, (((1,), (1,)), ((), ())), preferred_element_type=jnp.float32)
        attention = (mixed[:, :head_dim] / mixed[:, head_dim : head_dim + 1]).astype(jnp.bfloat16)
        gated = jnp.where(live, gate * attention.astype(jnp.float32), 0.0).astype(jnp.bfloat16)
        for i, k in enumerate(cols):
            out_0[:, k] = gated[2 * i * rows : (2 * i + 1) * rows]
            out_1[:, k] = gated[(2 * i + 1) * rows : (2 * i + 2) * rows]


def attend(scalars, gate, kv, q_0, q_1, held, head_dim, whole, chunk):
    rows, width = q_1.shape[1:]
    tokens = kv.shape[-1]
    piece = pl.BlockSpec((rows, width), lambda i, s: (0, 0))
    q_piece = pl.BlockSpec((pl.Squeezed(), rows, width), lambda i, s: (chunk, 0, 0))
    column = pl.BlockSpec((rows, width), lambda i, s: (0, s[0]))
    grid_spec = pltpu.PrefetchScalarGridSpec(
        num_scalar_prefetch=1,
        grid=(1,),
        in_specs=[
            pl.BlockSpec(memory_space=pltpu.SMEM),
            pl.BlockSpec(kv.shape, lambda i, s: (0, 0, 0)),
            column if whole else q_piece,
            q_piece,
            pl.BlockSpec(memory_space=pl.ANY),
        ],
        out_specs=[column if whole else piece, piece],
    )
    n_q = 2 * rows * width // head_dim
    return pl.pallas_call(
        functools.partial(attend_kernel, head_dim),
        out_shape=[
            jax.ShapeDtypeStruct(q_0.shape if whole else (rows, width), jnp.bfloat16),
            jax.ShapeDtypeStruct((rows, width), jnp.bfloat16),
        ],
        grid_spec=grid_spec,
        input_output_aliases={5: 0} if whole == 2 else {},
        compiler_params=params(28),
        cost_estimate=pl.CostEstimate(
            flops=4 * n_q * tokens * head_dim, bytes_accessed=4 << 20, transcendentals=n_q * tokens
        ),
        name="attend",
    )(scalars, gate, kv, q_0, q_1, held)


def place_kernel(scalars, *refs):
    n = len(refs) - 3
    received, out, sems = refs[:n], refs[n + 1], refs[n + 2]
    width = received[0].shape[1]
    copies = []
    for i in range(n):
        cols = pl.ds(pl.multiple_of(scalars[i] * width, width), width)
        copies.append(pltpu.make_async_copy(received[i], out.at[:, cols], sems.at[i]))
    for copy in copies:
        copy.start()
    for copy in copies:
        copy.wait()


def place(columns, received, held):
    n = len(received)
    return pl.pallas_call(
        place_kernel,
        out_shape=jax.ShapeDtypeStruct(held.shape, held.dtype),
        in_specs=[pl.BlockSpec(memory_space=pltpu.SMEM)]
        + [pl.BlockSpec(memory_space=pltpu.VMEM)] * n
        + [pl.BlockSpec(memory_space=pl.ANY)],
        out_specs=pl.BlockSpec(memory_space=pl.ANY),
        scratch_shapes=[pltpu.SemaphoreType.DMA((n,))],
        input_output_aliases={n + 1: 0},
        compiler_params=params(8),
        cost_estimate=pl.CostEstimate(flops=0, bytes_accessed=1 << 20, transcendentals=0),
        name="place",
    )(jnp.stack(columns).astype(jnp.int32), *received, held)


def on_device(queries, image_tokens, kv_weight, attn_gate, image_counts, response_lengths):
    rows = queries.shape[1]
    head_dim = kv_weight.shape[3]
    width = queries.shape[2] // 8
    z, xh, y, c = (lax.axis_index(a) for a in (Z, XH, Y, C))
    xl = lax.axis_index(XL)
    q = queries[0]
    image = image_tokens[0].T
    w_own = kv_weight[:, 0].transpose(1, 2, 0).reshape(2 * head_dim, -1)

    others = ((1, 0), (1, 1), (0, 1))

    def to_other(value, dx, dc):
        return lax.ppermute(value, (XH, C), [(i, i ^ (dx * 2 + dc)) for i in range(4)])

    def column_of(dx, dc, chunk):
        step = jnp.where((xh ^ dx) == 0, chunk, 3 - chunk)
        return (c ^ dc) * 4 + (z + step) % 4

    def position_of(dx, dc):
        return (((xh ^ dx) * 4 + y) * 2 + (c ^ dc)) * rows

    def query_slice(dx, dc):
        cut = [lax.dynamic_slice_in_dim(q, column_of(dx, dc, chunk) * width, width, axis=1) for chunk in (0, 1)]
        return jnp.stack(cut)

    def exchange(values):
        return [to_other(value, dx, dc) for value, (dx, dc) in zip(values, others)]

    firsts = [lax.ppermute(w_own, (XL, Z, C), weight_round(flip)) for flip in range(2)]
    image_other = lax.ppermute(image, C, ring(2, 1))
    swapped = (xl ^ c) == 1
    stack = jnp.stack([jnp.where(swapped, firsts[1], firsts[0]), jnp.where(swapped, firsts[0], firsts[1])])
    w_prev = lax.ppermute(stack, Z, ring(4, 1))
    w_next = lax.ppermute(stack, Z, ring(4, -1))
    w_far = lax.ppermute(stack, Z, ring(4, 2))
    q_got = exchange([query_slice(dx, dc) for dx, dc in others])

    count = image_counts[0]
    sum_info = jnp.stack([count, (y < 2).astype(jnp.int32)])
    gate = jnp.tanh(attn_gate)

    parts_0 = project(stack, image, image_other, 0, w_own)
    parts_0 = project(w_prev, image, image_other, 1, parts_0)
    parts_0, w_next, q_got = lax.optimization_barrier((parts_0, w_next, q_got))
    parts_0 = lax.all_to_all(parts_0, CHIPS, 0, 0, tiled=True)
    parts_1 = project(w_next, image, image_other, 0, w_own)
    parts_1 = project(w_far, image, image_other, 1, parts_1)
    parts_1, parts_0 = lax.optimization_barrier((parts_1, parts_0))
    parts_1 = lax.all_to_all(parts_1, CHIPS, 0, 0, tiled=True)
    sum_0 = sum_parts(sum_info, parts_0)
    sum_0, parts_1 = lax.optimization_barrier((sum_0, parts_1))
    kv_0 = lax.all_to_all(sum_0, Y, 0, 0, tiled=True)
    sum_1 = sum_parts(sum_info, parts_1)
    kv_1 = lax.all_to_all(sum_1, Y, 0, 0, tiled=True)

    def scalars_of(chunk, groups):
        values = [column_of(0, 0, chunk), count] + [position_of(*g) for g in groups] + [response_lengths[0]]
        return jnp.stack(values).astype(jnp.int32)

    out = None
    for chunk, kv in enumerate((kv_0, kv_1)):
        far, far_other, near = q_got
        scalars = scalars_of(chunk, others[:2])
        give = attend(scalars, gate, kv, far, far_other, near if out is None else out, head_dim, 0, chunk)
        held = give[0] if out is None else out
        scalars = scalars_of(chunk, ((0, 0), (0, 1)))
        out, give_near = attend(scalars, gate, kv, q, near, held, head_dim, 1 if out is None else 2, chunk)
        got = exchange([give[0], give[1], give_near])
        out = place([column_of(dx, dc, chunk) for dx, dc in others], got, out)
    return out[None]


def solution(mesh):
    fine = Mesh(mesh.devices.reshape(2, 4, 2, 4, 2), (XL, Z, XH, Y, C))
    sample, head = (XL, Z), (XH, Y, C)
    placed = (
        P(sample, head, None),
        P(sample, None, head),
        P(head, sample, None, None),
        P(),
        P(sample),
        P(sample),
    )
    return jax.shard_map(
        on_device, mesh=fine, in_specs=placed, out_specs=P(sample, head, None), check_vma=False
    )
```

```python
import functools

import jax
import jax.numpy as jnp
from jax import lax
from jax.experimental import pallas as pl
from jax.experimental.pallas import tpu as pltpu
from jax.sharding import Mesh
from jax.sharding import PartitionSpec as P

XL, Z, XH, Y, C = "xl", "z", "xh", "y", "c"
CHIPS = (XH, Y)
N_CHIPS = 8
MIB = 1024 * 1024


IN_VMEM = pl.BlockSpec(memory_space=pltpu.VMEM)
IN_SMEM = pl.BlockSpec(memory_space=pltpu.SMEM)
IN_HBM = pl.BlockSpec(memory_space=pltpu.HBM)


def params(mib):
    return pltpu.CompilerParams(vmem_limit_bytes=mib * MIB)


def weight_round(flip):
    pairs = []
    for xl in range(2):
        for z in range(4):
            for b in range(2):
                pairs.append(((xl * 4 + z) * 2 + b, ((b ^ flip) * 4 + z) * 2 + xl))
    return pairs


def ring(size, step):
    return [(i, (i + step) % size) for i in range(size)]


def project_kernel(side, swap_ref, w_ref, own_ref, other_ref, held, out_ref, buffer, sem):
    del held
    swap = swap_ref[0] == 1
    w_0, w_1 = w_ref[0], w_ref[1]
    acc = jnp.dot(jnp.where(swap, w_1, w_0), own_ref[...], preferred_element_type=jnp.float32)
    acc += jnp.dot(jnp.where(swap, w_0, w_1), other_ref[...], preferred_element_type=jnp.float32)
    buffer[...] = acc.astype(jnp.bfloat16).reshape(buffer.shape)
    groups = buffer.shape[0]
    copy = pltpu.make_async_copy(buffer, out_ref.at[pl.ds(side * groups, groups)], sem)
    copy.start()
    copy.wait()


def project(swap, weight, own_image, other_image, side, held):
    kv_rows = weight.shape[1]
    depth, tokens = own_image.shape
    groups = N_CHIPS // 2
    shape = (N_CHIPS, kv_rows // groups, tokens)
    return pl.pallas_call(
        functools.partial(project_kernel, side),
        out_shape=pltpu.HBM(shape, jnp.bfloat16),
        in_specs=[IN_SMEM] + [IN_VMEM] * 3 + [IN_HBM],
        out_specs=IN_HBM,
        scratch_shapes=[pltpu.VMEM((groups,) + shape[1:], jnp.bfloat16), pltpu.SemaphoreType.DMA],
        input_output_aliases={4: 0} if held.shape == shape else {},
        compiler_params=params(20),
        cost_estimate=pl.CostEstimate(
            flops=2 * kv_rows * tokens * depth * 2, bytes_accessed=5 * MIB, transcendentals=0
        ),
        name="project",
    )(swap, weight, own_image, other_image, held)


def sum_kernel(info_ref, parts_ref, out_ref, buffer, sems):
    n = parts_ref.shape[0]
    copies = [pltpu.make_async_copy(parts_ref.at[d], buffer.at[d], sems.at[d]) for d in range(n)]
    for copy in copies:
        copy.start()
    copies[0].wait()
    total = buffer[0].astype(jnp.float32)
    for d in range(1, n):
        copies[d].wait()
        total += buffer[d].astype(jnp.float32)
    first = jnp.where(info_ref[1] == 1, total[:, :1], 0.0)
    slot = lax.broadcasted_iota(jnp.int32, total.shape, 1)
    out_ref[...] = jnp.where(slot < info_ref[0], total, first).astype(jnp.bfloat16)


def sum_parts(info, parts):
    n = parts.shape[0]
    return pl.pallas_call(
        sum_kernel,
        out_shape=jax.ShapeDtypeStruct(parts.shape[1:], jnp.bfloat16),
        in_specs=[IN_SMEM, IN_HBM],
        out_specs=IN_VMEM,
        scratch_shapes=[pltpu.VMEM(parts.shape, jnp.bfloat16), pltpu.SemaphoreType.DMA((n,))],
        compiler_params=params(16),
        cost_estimate=pl.CostEstimate(flops=1 << 20, bytes_accessed=2 * MIB, transcendentals=0),
        name="sum_parts",
    )(info, pltpu.with_memory_space_constraint(parts, pltpu.HBM))


def attend_kernel(head_dim, whole, jobs, scalars, gate_ref, *refs):
    n_jobs, n_groups = len(jobs), len(jobs[0])
    pieces, refs = refs[: 4 * n_jobs], refs[4 * n_jobs :]
    q_refs, refs = refs[: n_jobs * n_groups], refs[n_jobs * n_groups + 1 :]
    outs, (kv, queries, own_out, sems, out_sems) = refs[:-5], refs[-5:]
    rows, width = own_out.shape[1:]
    tokens = kv.shape[2]
    piece_rows = pieces[0].shape[0]
    copies, columns = [], []
    for j in range(n_jobs):
        base = 2 + n_groups + 5 * j
        columns.append(pl.ds(pl.multiple_of(scalars[base] * width, width), width))
        now = []
        for i in range(n_groups):
            ref = q_refs[j * n_groups + i]
            source = ref.at[:, columns[j]] if whole and i == 0 else ref.at[jobs[j][i]]
            now.append((source, queries.at[j, i]))
        for d in range(4):
            to = pl.ds(pl.multiple_of(scalars[base + 1 + d], piece_rows), piece_rows)
            now.append((pieces[4 * j + d], kv.at[j, to]))
        copies.append([pltpu.make_async_copy(*pair, sems.at[j, n]) for n, pair in enumerate(now)])
    for copy in sum(copies, []):
        copy.start()

    slot = lax.broadcasted_iota(jnp.int32, (head_dim, tokens), 1)
    row = lax.broadcasted_iota(jnp.int32, (head_dim, tokens), 0)
    counted = ((slot < scalars[0]) & (row == 0)).astype(jnp.float32).astype(jnp.bfloat16)
    gate = gate_ref[0]
    factor = head_dim**-0.5 * 1.4426950408889634
    heads = 4 // n_groups
    live = []
    for i in range(n_groups):
        live.append(scalars[2 + i] + lax.broadcasted_iota(jnp.int32, (rows, head_dim), 0) < scalars[1])
    live = jnp.concatenate(live * heads, axis=0)
    stores = []
    for j in range(n_jobs):
        for copy in copies[j]:
            copy.wait()
        keys = kv[j, :head_dim]
        values = jnp.concatenate([kv[j, head_dim:], counted], axis=0)
        for h in range(0, width // head_dim, heads):
            parts = [(i, slice(k * head_dim, (k + 1) * head_dim)) for k in range(h, h + heads) for i in range(n_groups)]
            q = jnp.concatenate([queries[j, i, :, cols] for i, cols in parts], axis=0)
            scores = jnp.dot(q, keys, preferred_element_type=jnp.float32)
            top = jnp.max(scores, axis=1, keepdims=True) * factor
            weights = jnp.exp2(scores * factor - top).astype(jnp.bfloat16)
            mixed = lax.dot_general(weights, values, (((1,), (1,)), ((), ())), preferred_element_type=jnp.float32)
            attention = (mixed[:, :head_dim] / mixed[:, head_dim : head_dim + 1]).astype(jnp.bfloat16)
            gated = jnp.where(live, gate * attention.astype(jnp.float32), 0.0).astype(jnp.bfloat16)
            for n, (i, cols) in enumerate(parts):
                value = gated[n * rows : (n + 1) * rows]
                if whole and i == 0:
                    own_out[j, :, cols] = value
                else:
                    outs[i][j, :, cols] = value
        if whole:
            stores.append(pltpu.make_async_copy(own_out.at[j], outs[0].at[:, columns[j]], out_sems.at[j]))
            stores[-1].start()
    for store in stores:
        store.wait()


def attend(scalars, gate, jobs, held, head_dim, whole):
    n_jobs, n = len(jobs), len(jobs[0][1])
    pieces = [x for kv, _ in jobs for x in kv]
    arrays = [x for _, queries in jobs for x, _ in queries]
    places = [[i for _, i in queries] for _, queries in jobs]
    rows, width = arrays[-1].shape[1:]
    tokens = pieces[0].shape[-1]
    shapes = [jax.ShapeDtypeStruct((n_jobs, rows, width), jnp.bfloat16)] * n
    if whole:
        shapes[0] = pltpu.HBM(arrays[0].shape, jnp.bfloat16)
    n_q = n_jobs * n * rows * width // head_dim
    return pl.pallas_call(
        functools.partial(attend_kernel, head_dim, whole, places),
        out_shape=shapes,
        in_specs=[IN_SMEM, IN_SMEM] + [IN_HBM] * (len(pieces) + len(arrays) + 1),
        out_specs=[IN_HBM if whole and i == 0 else IN_VMEM for i in range(n)],
        scratch_shapes=[
            pltpu.VMEM((n_jobs, 2 * head_dim, tokens), jnp.bfloat16),
            pltpu.VMEM((n_jobs, n, rows, width), jnp.bfloat16),
            pltpu.VMEM((n_jobs, rows, width), jnp.bfloat16),
            pltpu.SemaphoreType.DMA((n_jobs, n + 4)),
            pltpu.SemaphoreType.DMA((n_jobs,)),
        ],
        input_output_aliases={2 + len(pieces) + len(arrays): 0} if whole and held.shape == arrays[0].shape else {},
        compiler_params=params(28),
        cost_estimate=pl.CostEstimate(
            flops=4 * n_q * tokens * head_dim, bytes_accessed=4 * MIB, transcendentals=n_q * tokens
        ),
        name="attend",
    )(scalars, gate, *pieces, *arrays, held)


def place_kernel(jobs, scalars, *refs):
    out, sems = refs[-2:]
    copies = []
    for n, (i, part) in enumerate(jobs):
        width = refs[i].shape[2]
        cols = pl.ds(pl.multiple_of(scalars[n] * width, width), width)
        copies.append(pltpu.make_async_copy(refs[i].at[part], out.at[:, cols], sems.at[n]))
    for copy in copies:
        copy.start()
    for copy in copies:
        copy.wait()


def place(columns, received, held):
    n = len(received)
    jobs = [(i, part) for i, x in enumerate(received) for part in range(x.shape[0])]
    return pl.pallas_call(
        functools.partial(place_kernel, jobs),
        out_shape=jax.ShapeDtypeStruct(held.shape, held.dtype),
        in_specs=[IN_SMEM] + [IN_VMEM] * n + [IN_HBM],
        out_specs=IN_HBM,
        scratch_shapes=[pltpu.SemaphoreType.DMA((len(jobs),))],
        input_output_aliases={n + 1: 0},
        compiler_params=params(8),
        cost_estimate=pl.CostEstimate(flops=0, bytes_accessed=1 << 20, transcendentals=0),
        name="place",
    )(jnp.stack(columns).astype(jnp.int32), *received, held)


def on_device(queries, image_tokens, kv_weight, attn_gate, image_counts, response_lengths):
    rows = queries.shape[1]
    head_dim = kv_weight.shape[3]
    width = queries.shape[2] // 8
    z, xh, y, c = (lax.axis_index(a) for a in (Z, XH, Y, C))
    xl = lax.axis_index(XL)
    q = queries[0]
    image = image_tokens[0].T
    w_own = kv_weight[:, 0].transpose(1, 2, 0).reshape(2 * head_dim, -1)

    others = ((1, 0), (1, 1), (0, 1))

    def to_other(value, dx, dc):
        return lax.ppermute(value, (XH, C), [(i, i ^ (dx * 2 + dc)) for i in range(4)])

    def column_of(dx, dc, chunk):
        step = jnp.where((xh ^ dx) == 0, chunk, 3 - chunk)
        return (c ^ dc) * 4 + (z + step) % 4

    def position_of(dx, dc):
        return (((xh ^ dx) * 4 + y) * 2 + (c ^ dc)) * rows

    def query_slice(dx, dc, chunk):
        return lax.dynamic_slice_in_dim(q, column_of(dx, dc, chunk) * width, width, axis=1)[None]

    def exchange(values):
        return [to_other(value, dx, dc) for value, (dx, dc) in zip(values, others)]

    w_here = jnp.stack([lax.ppermute(w_own, (XL, Z, C), weight_round(flip)) for flip in range(2)])
    image_other = lax.ppermute(image, C, ring(2, 1))
    w_prev = lax.ppermute(w_here, Z, ring(4, 1))
    w_next = lax.ppermute(w_here, Z, ring(4, -1))
    w_far = lax.ppermute(w_here, Z, ring(4, 2))
    swap = (xl ^ c).astype(jnp.int32).reshape(1)

    count = image_counts[0]
    sum_info = jnp.stack([count, (y < 2).astype(jnp.int32)])
    gate = jnp.tanh(attn_gate)

    parts_0 = project(swap, w_here, image, image_other, 0, w_own)
    parts_0 = project(swap, w_prev, image, image_other, 1, parts_0)
    here, far, far_other, near = (0, 0), *others

    def in_hbm(x):
        return pltpu.with_memory_space_constraint(x, pltpu.HBM)

    q_far_0 = to_other(query_slice(*far, 0), *far)
    q_near = to_other(jnp.concatenate([query_slice(*near, chunk) for chunk in (0, 1)]), *near)
    parts_0, q_far_0, w_next = lax.optimization_barrier((parts_0, q_far_0, w_next))
    parts_0 = lax.all_to_all(parts_0, CHIPS, 0, 0, tiled=True)
    parts_1 = project(swap, w_next, image, image_other, 0, w_own)
    parts_1 = project(swap, w_far, image, image_other, 1, parts_1)
    parts_1, parts_0, q_near, q_send = lax.optimization_barrier((parts_1, parts_0, q_near, query_slice(*far_other, 0)))
    parts_1 = lax.all_to_all(parts_1, CHIPS, 0, 0, tiled=True)
    sum_0 = sum_parts(sum_info, parts_0)
    kv_0 = [sum_0] + [lax.ppermute(sum_0, Y, ring(4, step)) for step in (1, 3, 2)]
    q_far_other_0 = to_other(q_send, *far_other)
    sum_1 = sum_parts(sum_info, parts_1)
    kv_1 = [sum_1] + [lax.ppermute(sum_1, Y, ring(4, step)) for step in (1, 3, 2)]
    q_send, sum_1 = lax.optimization_barrier(([query_slice(*other, 1) for other in (far, far_other)], sum_1))
    q_far_1, q_far_other_1 = (to_other(x, *other) for x, other in zip(q_send, (far, far_other)))

    pieces_at = [(y - step) % 4 * (2 * head_dim // 4) for step in (0, 1, 3, 2)]

    def scalars_of(chunks, groups):
        values = [count, response_lengths[0]] + [position_of(*g) for g in groups]
        for chunk in chunks:
            values += [column_of(0, 0, chunk)] + pieces_at
        return jnp.stack(values).astype(jnp.int32)

    groups = (far, far_other)
    kv_0 = [in_hbm(x) for x in kv_0]
    q_0 = [(in_hbm(x), 0) for x in (q_far_0, q_far_other_0)]
    gives_0 = attend(scalars_of((0,), groups), gate, [(kv_0, q_0)], w_own, head_dim, False)
    q_1 = [(x, 0) for x in (q_far_1, q_far_other_1)]
    gives_1 = attend(scalars_of((1,), groups), gate, [(kv_1, q_1)], gives_0[0], head_dim, False)
    got = [to_other(value, *other) for gives in (gives_0, gives_1) for value, other in zip(gives, groups)]
    columns = [column_of(*other, chunk) for chunk in (0, 1) for other in groups]
    q_near = in_hbm(q_near)
    out = gives_1[0]
    for chunk, kv in enumerate((kv_0, kv_1)):
        job = (kv, [(q, 0), (q_near, chunk)])
        out, give = attend(scalars_of((chunk,), (here, near)), gate, [job], out, head_dim, True)
        got.append(to_other(give, *near))
        columns.append(column_of(*near, chunk))
    out = place(columns, got, out)
    return out[None]


def solution(mesh):
    fine = Mesh(mesh.devices.reshape(2, 4, 2, 4, 2), (XL, Z, XH, Y, C))
    sample, head = (XL, Z), (XH, Y, C)
    placed = (
        P(sample, head, None),
        P(sample, None, head),
        P(head, sample, None, None),
        P(),
        P(sample),
        P(sample),
    )
    return jax.shard_map(
        on_device, mesh=fine, in_specs=placed, out_specs=P(sample, head, None), check_vma=False
    )
```

```python
import functools

import jax
import jax.numpy as jnp
from jax import lax
from jax.experimental import pallas as pl
from jax.experimental.pallas import tpu as pltpu
from jax.sharding import Mesh
from jax.sharding import PartitionSpec as P

XL, Z, XH, Y, C = "xl", "z", "xh", "y", "c"
CHIPS = (XH, Y)
N_CHIPS = 8
MIB = 1024 * 1024


IN_VMEM = pl.BlockSpec(memory_space=pltpu.VMEM)
IN_SMEM = pl.BlockSpec(memory_space=pltpu.SMEM)
IN_HBM = pl.BlockSpec(memory_space=pltpu.HBM)


def params(mib):
    return pltpu.CompilerParams(vmem_limit_bytes=mib * MIB)


def weight_round(flip):
    pairs = []
    for xl in range(2):
        for z in range(4):
            for b in range(2):
                pairs.append(((xl * 4 + z) * 2 + b, ((b ^ flip) * 4 + z) * 2 + xl))
    return pairs


def ring(size, step):
    return [(i, (i + step) % size) for i in range(size)]


def project_kernel(side, swap_ref, w_ref, own_ref, other_ref, held, out_ref, buffer, sem):
    del held
    swap = swap_ref[0] == 1
    w_0, w_1 = w_ref[0], w_ref[1]
    acc = jnp.dot(jnp.where(swap, w_1, w_0), own_ref[...], preferred_element_type=jnp.float32)
    acc += jnp.dot(jnp.where(swap, w_0, w_1), other_ref[...], preferred_element_type=jnp.float32)
    buffer[...] = acc.astype(jnp.bfloat16).reshape(buffer.shape)
    groups = buffer.shape[0]
    copy = pltpu.make_async_copy(buffer, out_ref.at[pl.ds(side * groups, groups)], sem)
    copy.start()
    copy.wait()


def project(swap, weight, own_image, other_image, side, held):
    kv_rows = weight.shape[1]
    depth, tokens = own_image.shape
    groups = N_CHIPS // 2
    shape = (N_CHIPS, kv_rows // groups, tokens)
    return pl.pallas_call(
        functools.partial(project_kernel, side),
        out_shape=pltpu.HBM(shape, jnp.bfloat16),
        in_specs=[IN_SMEM] + [IN_VMEM] * 3 + [IN_HBM],
        out_specs=IN_HBM,
        scratch_shapes=[pltpu.VMEM((groups,) + shape[1:], jnp.bfloat16), pltpu.SemaphoreType.DMA],
        input_output_aliases={4: 0} if held.shape == shape else {},
        compiler_params=params(20),
        cost_estimate=pl.CostEstimate(
            flops=2 * kv_rows * tokens * depth * 2, bytes_accessed=5 * MIB, transcendentals=0
        ),
        name="project",
    )(swap, weight, own_image, other_image, held)


def sum_kernel(info_ref, parts_ref, out_ref):
    total = parts_ref[0].astype(jnp.float32)
    for d in range(1, parts_ref.shape[0]):
        total += parts_ref[d].astype(jnp.float32)
    first = jnp.where(info_ref[1] == 1, total[:, :1], 0.0)
    slot = lax.broadcasted_iota(jnp.int32, total.shape, 1)
    out_ref[...] = jnp.where(slot < info_ref[0], total, first).astype(jnp.bfloat16)


def sum_parts(info, parts):
    return pl.pallas_call(
        sum_kernel,
        out_shape=jax.ShapeDtypeStruct(parts.shape[1:], jnp.bfloat16),
        in_specs=[IN_SMEM, IN_VMEM],
        out_specs=IN_VMEM,
        compiler_params=params(16),
        cost_estimate=pl.CostEstimate(flops=1 << 20, bytes_accessed=2 * MIB, transcendentals=0),
        name="sum_parts",
    )(info, parts)


def attend_kernel(head_dim, whole, jobs, base, scalars, gate_ref, *refs):
    n_jobs, n_groups = len(jobs), len(jobs[0])
    pieces, refs = refs[: 4 * n_jobs], refs[4 * n_jobs :]
    q_refs, refs = refs[: n_jobs * n_groups], refs[n_jobs * n_groups + 1 :]
    outs, (kv, queries, own_out, sems, out_sems) = refs[:-5], refs[-5:]
    rows, width = own_out.shape[1:]
    tokens = kv.shape[2]
    piece_rows = pieces[0].shape[0]
    copies, columns = [], []
    for j in range(n_jobs):
        at = base + 2 + n_groups + 5 * j
        columns.append(pl.ds(pl.multiple_of(scalars[at] * width, width), width))
        now = []
        for i in range(n_groups):
            ref = q_refs[j * n_groups + i]
            source = ref.at[:, columns[j]] if whole and i == 0 else ref.at[jobs[j][i]]
            now.append((source, queries.at[j, i]))
        for d in range(4):
            to = pl.ds(pl.multiple_of(scalars[at + 1 + d], piece_rows), piece_rows)
            now.append((pieces[4 * j + d], kv.at[j, to]))
        copies.append([pltpu.make_async_copy(*pair, sems.at[j, n]) for n, pair in enumerate(now)])
    for copy in sum(copies, []):
        copy.start()

    slot = lax.broadcasted_iota(jnp.int32, (head_dim, tokens), 1)
    row = lax.broadcasted_iota(jnp.int32, (head_dim, tokens), 0)
    counted = ((slot < scalars[base]) & (row == 0)).astype(jnp.float32).astype(jnp.bfloat16)
    gate = gate_ref[0]
    factor = head_dim**-0.5 * 1.4426950408889634
    heads = 4 // n_groups
    live = []
    for i in range(n_groups):
        live.append(scalars[base + 2 + i] + lax.broadcasted_iota(jnp.int32, (rows, head_dim), 0) < scalars[base + 1])
    live = jnp.concatenate(live * heads, axis=0)
    stores = []
    for j in range(n_jobs):
        for copy in copies[j]:
            copy.wait()
        keys = kv[j, :head_dim]
        values = jnp.concatenate([kv[j, head_dim:], counted], axis=0)
        for h in range(0, width // head_dim, heads):
            parts = [(i, slice(k * head_dim, (k + 1) * head_dim)) for k in range(h, h + heads) for i in range(n_groups)]
            q = jnp.concatenate([queries[j, i, :, cols] for i, cols in parts], axis=0)
            scores = jnp.dot(q, keys, preferred_element_type=jnp.float32)
            top = jnp.max(scores, axis=1, keepdims=True) * factor
            weights = jnp.exp2(scores * factor - top).astype(jnp.bfloat16)
            mixed = lax.dot_general(weights, values, (((1,), (1,)), ((), ())), preferred_element_type=jnp.float32)
            attention = (mixed[:, :head_dim] / mixed[:, head_dim : head_dim + 1]).astype(jnp.bfloat16)
            gated = jnp.where(live, gate * attention.astype(jnp.float32), 0.0).astype(jnp.bfloat16)
            for n, (i, cols) in enumerate(parts):
                value = gated[n * rows : (n + 1) * rows]
                if whole and i == 0:
                    own_out[j, :, cols] = value
                else:
                    outs[i][:, cols] = value
        if whole:
            stores.append(pltpu.make_async_copy(own_out.at[j], outs[0].at[:, columns[j]], out_sems.at[j]))
            stores[-1].start()
    for store in stores:
        store.wait()


def attend(scalars, base, gate, jobs, held, head_dim, whole):
    n_jobs, n = len(jobs), len(jobs[0][1])
    pieces = [x for kv, _ in jobs for x in kv]
    arrays = [x for _, queries in jobs for x, _ in queries]
    places = [[i for _, i in queries] for _, queries in jobs]
    rows, width = arrays[-1].shape[1:]
    tokens = pieces[0].shape[-1]
    shapes = [jax.ShapeDtypeStruct((rows, width), jnp.bfloat16)] * n
    if whole:
        shapes[0] = pltpu.HBM(arrays[0].shape, jnp.bfloat16)
    n_q = n_jobs * n * rows * width // head_dim
    return pl.pallas_call(
        functools.partial(attend_kernel, head_dim, whole, places, base),
        out_shape=shapes,
        in_specs=[IN_SMEM, IN_SMEM] + [IN_HBM] * (len(pieces) + len(arrays) + 1),
        out_specs=[IN_HBM if whole and i == 0 else IN_VMEM for i in range(len(shapes))],
        scratch_shapes=[
            pltpu.VMEM((n_jobs, 2 * head_dim, tokens), jnp.bfloat16),
            pltpu.VMEM((n_jobs, n, rows, width), jnp.bfloat16),
            pltpu.VMEM((n_jobs, rows, width), jnp.bfloat16),
            pltpu.SemaphoreType.DMA((n_jobs, n + 4)),
            pltpu.SemaphoreType.DMA((n_jobs,)),
        ],
        input_output_aliases={2 + len(pieces) + len(arrays): 0} if whole and held.shape == arrays[0].shape else {},
        compiler_params=params(28),
        cost_estimate=pl.CostEstimate(
            flops=4 * n_q * tokens * head_dim, bytes_accessed=4 * MIB, transcendentals=n_q * tokens
        ),
        name="attend",
    )(scalars, gate, *pieces, *arrays, held)


def place_kernel(base, scalars, *refs):
    *received, _, out, sems = refs
    copies = []
    for n, ref in enumerate(received):
        width = ref.shape[1]
        cols = pl.ds(pl.multiple_of(scalars[base + n] * width, width), width)
        copies.append(pltpu.make_async_copy(ref, out.at[:, cols], sems.at[n]))
    for copy in copies:
        copy.start()
    for copy in copies:
        copy.wait()


def place(scalars, base, received, held):
    n = len(received)
    return pl.pallas_call(
        functools.partial(place_kernel, base),
        out_shape=jax.ShapeDtypeStruct(held.shape, held.dtype),
        in_specs=[IN_SMEM] + [IN_VMEM] * n + [IN_HBM],
        out_specs=IN_HBM,
        scratch_shapes=[pltpu.SemaphoreType.DMA((n,))],
        input_output_aliases={n + 1: 0},
        compiler_params=params(8),
        cost_estimate=pl.CostEstimate(flops=0, bytes_accessed=1 << 20, transcendentals=0),
        name="place",
    )(scalars, *received, held)


def on_device(queries, image_tokens, kv_weight, attn_gate, image_counts, response_lengths):
    rows = queries.shape[1]
    head_dim = kv_weight.shape[3]
    width = queries.shape[2] // 8
    z, xh, y, c = (lax.axis_index(a) for a in (Z, XH, Y, C))
    xl = lax.axis_index(XL)
    q = queries[0]
    image = image_tokens[0].T
    w_own = kv_weight[:, 0].transpose(1, 2, 0).reshape(2 * head_dim, -1)

    others = ((1, 0), (1, 1), (0, 1))

    def to_other(value, dx, dc):
        return lax.ppermute(value, (XH, C), [(i, i ^ (dx * 2 + dc)) for i in range(4)])

    def column_of(dx, dc, chunk):
        step = jnp.where((xh ^ dx) == 0, chunk, 3 - chunk)
        return (c ^ dc) * 4 + (z + step) % 4

    def position_of(dx, dc):
        return (((xh ^ dx) * 4 + y) * 2 + (c ^ dc)) * rows

    def query_slice(dx, dc, chunk):
        return lax.dynamic_slice_in_dim(q, column_of(dx, dc, chunk) * width, width, axis=1)[None]

    def exchange(values):
        return [to_other(value, dx, dc) for value, (dx, dc) in zip(values, others)]

    w_here = jnp.stack([lax.ppermute(w_own, (XL, Z, C), weight_round(flip)) for flip in range(2)])
    image_other = lax.ppermute(image, C, ring(2, 1))
    w_prev = lax.ppermute(w_here, Z, ring(4, 1))
    w_next = lax.ppermute(w_here, Z, ring(4, -1))
    w_far = lax.ppermute(w_here, Z, ring(4, 2))
    swap = (xl ^ c).astype(jnp.int32).reshape(1)

    count = image_counts[0]
    sum_info = jnp.stack([count, (y < 2).astype(jnp.int32)])
    gate = jnp.tanh(attn_gate)

    parts_0 = project(swap, w_here, image, image_other, 0, w_own)
    parts_0 = project(swap, w_prev, image, image_other, 1, parts_0)
    here, far, far_other, near = (0, 0), *others

    def in_hbm(x):
        return pltpu.with_memory_space_constraint(x, pltpu.HBM)

    pieces_at = [(y - step) % 4 * (2 * head_dim // 4) for step in (0, 1, 3, 2)]
    groups = (far, far_other)
    values, base = [], {}
    for chunk in (0, 1):
        for name, now in (("far", groups), ("near", (here, near))):
            base[name, chunk] = len(values)
            values += [count, response_lengths[0]] + [position_of(*g) for g in now]
            values += [column_of(0, 0, chunk)] + pieces_at
    base["place"] = len(values)
    values += [column_of(*g, chunk) for chunk in (0, 1) for g in groups]
    values += [column_of(*near, chunk) for chunk in (0, 1)]
    scalars = jnp.stack(values).astype(jnp.int32)

    q_far_0 = to_other(query_slice(*far, 0), *far)
    q_near = to_other(jnp.concatenate([query_slice(*near, chunk) for chunk in (0, 1)]), *near)
    parts_0, q_far_0, w_next, scalars, sum_info, gate = lax.optimization_barrier(
        (parts_0, q_far_0, w_next, scalars, sum_info, gate)
    )
    parts_0 = lax.all_to_all(parts_0, CHIPS, 0, 0, tiled=True)
    parts_1 = project(swap, w_next, image, image_other, 0, w_own)
    parts_1 = project(swap, w_far, image, image_other, 1, parts_1)
    parts_1, parts_0, q_near, q_send = lax.optimization_barrier((parts_1, parts_0, q_near, query_slice(*far_other, 0)))
    parts_1 = lax.all_to_all(parts_1, CHIPS, 0, 0, tiled=True)
    sum_0 = sum_parts(sum_info, parts_0)
    kv_0 = [in_hbm(x) for x in [sum_0] + [lax.ppermute(sum_0, Y, ring(4, step)) for step in (1, 3, 2)]]
    q_far_other_0 = to_other(q_send, *far_other)

    sum_1 = sum_parts(sum_info, parts_1)
    kv_1 = [sum_1] + [lax.ppermute(sum_1, Y, ring(4, step)) for step in (1, 3, 2)]
    q_send, sum_1 = lax.optimization_barrier(([query_slice(*other, 1) for other in groups], sum_1))
    q_1 = [(to_other(x, *other), 0) for x, other in zip(q_send, groups)]

    q_near = in_hbm(q_near)
    q_0 = [(in_hbm(x), 0) for x in (q_far_0, q_far_other_0)]
    gives_0 = attend(scalars, base["far", 0], gate, [(kv_0, q_0)], w_own, head_dim, False)
    gives_1 = attend(scalars, base["far", 1], gate, [(kv_1, q_1)], gives_0[0], head_dim, False)
    got = [to_other(value, *other) for gives in (gives_0, gives_1) for value, other in zip(gives, groups)]
    out = gives_1[0]
    for chunk, kv in enumerate((kv_0, kv_1)):
        job = (kv, [(q, 0), (q_near, chunk)])
        out, give = attend(scalars, base["near", chunk], gate, [job], out, head_dim, True)
        got.append(to_other(give, *near))
    out = place(scalars, base["place"], got, out)
    return out[None]


def solution(mesh):
    fine = Mesh(mesh.devices.reshape(2, 4, 2, 4, 2), (XL, Z, XH, Y, C))
    sample, head = (XL, Z), (XH, Y, C)
    placed = (
        P(sample, head, None),
        P(sample, None, head),
        P(head, sample, None, None),
        P(),
        P(sample),
        P(sample),
    )
    return jax.shard_map(
        on_device, mesh=fine, in_specs=placed, out_specs=P(sample, head, None), check_vma=False
    )
```

```python
import functools

import jax
import jax.numpy as jnp
from jax import lax
from jax.experimental import pallas as pl
from jax.experimental.pallas import tpu as pltpu
from jax.sharding import Mesh
from jax.sharding import PartitionSpec as P

XL, Z, XH, Y, C = "xl", "z", "xh", "y", "c"
CHIPS = (XH, Y)
N_CHIPS = 8
MIB = 1024 * 1024


IN_VMEM = pl.BlockSpec(memory_space=pltpu.VMEM)
IN_SMEM = pl.BlockSpec(memory_space=pltpu.SMEM)
IN_HBM = pl.BlockSpec(memory_space=pltpu.HBM)


def params(mib):
    return pltpu.CompilerParams(vmem_limit_bytes=mib * MIB)


def weight_round(flip):
    pairs = []
    for xl in range(2):
        for z in range(4):
            for b in range(2):
                pairs.append(((xl * 4 + z) * 2 + b, ((b ^ flip) * 4 + z) * 2 + xl))
    return pairs


def ring(size, step):
    return [(i, (i + step) % size) for i in range(size)]


def project_kernel(side, swap_ref, w_ref, own_ref, other_ref, held, out_ref, buffer, sem):
    del held
    swap = swap_ref[0] == 1
    w_0, w_1 = w_ref[0], w_ref[1]
    acc = jnp.dot(jnp.where(swap, w_1, w_0), own_ref[...], preferred_element_type=jnp.float32)
    acc += jnp.dot(jnp.where(swap, w_0, w_1), other_ref[...], preferred_element_type=jnp.float32)
    buffer[...] = acc.astype(jnp.bfloat16).reshape(buffer.shape)
    groups = buffer.shape[0]
    copy = pltpu.make_async_copy(buffer, out_ref.at[pl.ds(side * groups, groups)], sem)
    copy.start()
    copy.wait()


def project(swap, weight, own_image, other_image, side, held):
    kv_rows = weight.shape[1]
    depth, tokens = own_image.shape
    groups = N_CHIPS // 2
    shape = (N_CHIPS, kv_rows // groups, tokens)
    return pl.pallas_call(
        functools.partial(project_kernel, side),
        out_shape=pltpu.HBM(shape, jnp.bfloat16),
        in_specs=[IN_SMEM] + [IN_VMEM] * 3 + [IN_HBM],
        out_specs=IN_HBM,
        scratch_shapes=[pltpu.VMEM((groups,) + shape[1:], jnp.bfloat16), pltpu.SemaphoreType.DMA],
        input_output_aliases={4: 0} if held.shape == shape else {},
        compiler_params=params(20),
        cost_estimate=pl.CostEstimate(
            flops=2 * kv_rows * tokens * depth * 2, bytes_accessed=5 * MIB, transcendentals=0
        ),
        name="project",
    )(swap, weight, own_image, other_image, held)


def sum_kernel(info_ref, parts_ref, out_ref):
    total = parts_ref[0].astype(jnp.float32)
    for d in range(1, parts_ref.shape[0]):
        total += parts_ref[d].astype(jnp.float32)
    first = jnp.where(info_ref[1] == 1, total[:, :1], 0.0)
    slot = lax.broadcasted_iota(jnp.int32, total.shape, 1)
    out_ref[...] = jnp.where(slot < info_ref[0], total, first).astype(jnp.bfloat16)


def sum_parts(info, parts):
    return pl.pallas_call(
        sum_kernel,
        out_shape=jax.ShapeDtypeStruct(parts.shape[1:], jnp.bfloat16),
        in_specs=[IN_SMEM, IN_VMEM],
        out_specs=IN_VMEM,
        compiler_params=params(16),
        cost_estimate=pl.CostEstimate(flops=1 << 20, bytes_accessed=2 * MIB, transcendentals=0),
        name="sum_parts",
    )(info, parts)


def attend_kernel(head_dim, whole, direct, jobs, base, scalars, gate_ref, *refs):
    n_jobs, n_groups = len(jobs), len(jobs[0])
    pieces, refs = refs[: 4 * n_jobs], refs[4 * n_jobs :]
    q_refs, refs = refs[: n_jobs * n_groups], refs[n_jobs * n_groups + 1 :]
    outs, (kv, queries, own_out, sems, out_sems) = refs[:-5], refs[-5:]
    rows, width = own_out.shape[1:]
    tokens = kv.shape[2]
    piece_rows = pieces[0].shape[0]
    copies, columns = [], []
    for j in range(n_jobs):
        at = base + 2 + n_groups + 5 * j
        columns.append(pl.ds(pl.multiple_of(scalars[at] * width, width), width))
        now = []
        for i in range(n_groups):
            ref = q_refs[j * n_groups + i]
            if not direct:
                now.append((ref.at[jobs[j][i]], queries.at[j, i]))
        for d in range(4):
            to = pl.ds(pl.multiple_of(scalars[at + 1 + d], piece_rows), piece_rows)
            if not direct:
                now.append((pieces[4 * j + d], kv.at[j, to]))
        copies.append([pltpu.make_async_copy(*pair, sems.at[j, n]) for n, pair in enumerate(now)])
    for copy in sum(copies, []):
        copy.start()
    if direct:
        for j in range(n_jobs):
            for d in range(4):
                to = pl.ds(pl.multiple_of(scalars[base + 3 + n_groups + 5 * j + d], piece_rows), piece_rows)
                kv[j, to] = pieces[4 * j + d][...]

    def query(j, i, cols):
        if direct:
            return q_refs[j * n_groups + i][jobs[j][i], :, cols]
        return queries[j, i, :, cols]

    slot = lax.broadcasted_iota(jnp.int32, (head_dim, tokens), 1)
    row = lax.broadcasted_iota(jnp.int32, (head_dim, tokens), 0)
    counted = ((slot < scalars[base]) & (row == 0)).astype(jnp.float32).astype(jnp.bfloat16)
    gate = gate_ref[0]
    factor = head_dim**-0.5 * 1.4426950408889634
    heads = 8 // n_groups
    live = []
    for i in range(n_groups):
        live.append(scalars[base + 2 + i] + lax.broadcasted_iota(jnp.int32, (rows, head_dim), 0) < scalars[base + 1])
    live = jnp.concatenate(live * heads, axis=0)
    stores = []
    for j in range(n_jobs):
        for copy in copies[j]:
            copy.wait()
        keys = kv[j, :head_dim]
        values = jnp.concatenate([kv[j, head_dim:], counted], axis=0)
        for h in range(0, width // head_dim, heads):
            parts = [(i, slice(k * head_dim, (k + 1) * head_dim)) for k in range(h, h + heads) for i in range(n_groups)]
            q = jnp.concatenate([query(j, i, cols) for i, cols in parts], axis=0)
            scores = jnp.dot(q, keys, preferred_element_type=jnp.float32)
            top = jnp.max(scores, axis=1, keepdims=True) * factor
            weights = jnp.exp2(scores * factor - top).astype(jnp.bfloat16)
            mixed = lax.dot_general(weights, values, (((1,), (1,)), ((), ())), preferred_element_type=jnp.float32)
            attention = (mixed[:, :head_dim] / mixed[:, head_dim : head_dim + 1]).astype(jnp.bfloat16)
            gated = jnp.where(live, gate * attention.astype(jnp.float32), 0.0).astype(jnp.bfloat16)
            for n, (i, cols) in enumerate(parts):
                value = gated[n * rows : (n + 1) * rows]
                if whole and i == 0:
                    own_out[j, :, cols] = value
                else:
                    outs[i][:, cols] = value
        if whole:
            stores.append(pltpu.make_async_copy(own_out.at[j], outs[0].at[:, columns[j]], out_sems.at[j]))
            stores[-1].start()
    for store in stores:
        store.wait()


def attend(scalars, base, gate, jobs, held, head_dim, whole, direct):
    n_jobs, n = len(jobs), len(jobs[0][1])
    pieces = [x for kv, _ in jobs for x in kv]
    arrays = [x for _, queries in jobs for x, _ in queries]
    places = [[i for _, i in queries] for _, queries in jobs]
    rows, width = arrays[-1].shape[1:]
    tokens = pieces[0].shape[-1]
    shapes = [jax.ShapeDtypeStruct((rows, width), jnp.bfloat16)] * n
    if whole:
        shapes[0] = pltpu.HBM(whole, jnp.bfloat16)
    n_q = n_jobs * n * rows * width // head_dim
    return pl.pallas_call(
        functools.partial(attend_kernel, head_dim, whole is not None, direct, places, base),
        out_shape=shapes,
        in_specs=[IN_SMEM, IN_SMEM]
        + [IN_VMEM if direct else IN_HBM] * len(pieces)
        + [IN_VMEM if direct else IN_HBM] * len(arrays)
        + [IN_HBM],
        out_specs=[IN_HBM if whole and i == 0 else IN_VMEM for i in range(len(shapes))],
        scratch_shapes=[
            pltpu.VMEM((n_jobs, 2 * head_dim, tokens), jnp.bfloat16),
            pltpu.VMEM((n_jobs, n, rows, width), jnp.bfloat16),
            pltpu.VMEM((n_jobs, rows, width), jnp.bfloat16),
            pltpu.SemaphoreType.DMA((n_jobs, n + 4)),
            pltpu.SemaphoreType.DMA((n_jobs,)),
        ],
        input_output_aliases={2 + len(pieces) + len(arrays): 0} if held.shape == whole else {},
        compiler_params=params(28),
        cost_estimate=pl.CostEstimate(
            flops=4 * n_q * tokens * head_dim, bytes_accessed=4 * MIB, transcendentals=n_q * tokens
        ),
        name="attend",
    )(scalars, gate, *pieces, *arrays, held)


def place_kernel(base, scalars, *refs):
    *received, _, out, sems = refs
    copies = []
    for n, ref in enumerate(received):
        width = ref.shape[1]
        cols = pl.ds(pl.multiple_of(scalars[base + n] * width, width), width)
        copies.append(pltpu.make_async_copy(ref, out.at[:, cols], sems.at[n]))
    for copy in copies:
        copy.start()
    for copy in copies:
        copy.wait()


def place(scalars, base, received, held):
    n = len(received)
    return pl.pallas_call(
        functools.partial(place_kernel, base),
        out_shape=jax.ShapeDtypeStruct(held.shape, held.dtype),
        in_specs=[IN_SMEM] + [IN_VMEM] * n + [IN_HBM],
        out_specs=IN_HBM,
        scratch_shapes=[pltpu.SemaphoreType.DMA((n,))],
        input_output_aliases={n + 1: 0},
        compiler_params=params(8),
        cost_estimate=pl.CostEstimate(flops=0, bytes_accessed=1 << 20, transcendentals=0),
        name="place",
    )(scalars, *received, held)


def on_device(queries, image_tokens, kv_weight, attn_gate, image_counts, response_lengths):
    rows = queries.shape[1]
    head_dim = kv_weight.shape[3]
    width = queries.shape[2] // 8
    z, xh, y, c = (lax.axis_index(a) for a in (Z, XH, Y, C))
    xl = lax.axis_index(XL)
    q = queries[0]
    image = image_tokens[0].T
    w_own = kv_weight[:, 0].transpose(1, 2, 0).reshape(2 * head_dim, -1)

    others = ((1, 0), (1, 1), (0, 1))

    def to_other(value, dx, dc):
        return lax.ppermute(value, (XH, C), [(i, i ^ (dx * 2 + dc)) for i in range(4)])

    def column_of(dx, dc, chunk):
        step = jnp.where((xh ^ dx) == 0, chunk, 3 - chunk)
        return (c ^ dc) * 4 + (z + step) % 4

    def position_of(dx, dc):
        return (((xh ^ dx) * 4 + y) * 2 + (c ^ dc)) * rows

    def query_slice(dx, dc, chunk):
        return lax.dynamic_slice_in_dim(q, column_of(dx, dc, chunk) * width, width, axis=1)[None]

    def exchange(values):
        return [to_other(value, dx, dc) for value, (dx, dc) in zip(values, others)]

    w_here = jnp.stack([lax.ppermute(w_own, (XL, Z, C), weight_round(flip)) for flip in range(2)])
    image_other = lax.ppermute(image, C, ring(2, 1))
    w_prev = lax.ppermute(w_here, Z, ring(4, 1))
    w_next = lax.ppermute(w_here, Z, ring(4, -1))
    w_far = lax.ppermute(w_here, Z, ring(4, 2))
    swap = (xl ^ c).astype(jnp.int32).reshape(1)

    count = image_counts[0]
    sum_info = jnp.stack([count, (y < 2).astype(jnp.int32)])
    gate = jnp.tanh(attn_gate)

    parts_0 = project(swap, w_here, image, image_other, 0, w_own)
    parts_0 = project(swap, w_prev, image, image_other, 1, parts_0)
    here, far, far_other, near = (0, 0), *others

    def in_hbm(x):
        return pltpu.with_memory_space_constraint(x, pltpu.HBM)

    pieces_at = [(y - step) % 4 * (2 * head_dim // 4) for step in (0, 1, 3, 2)]
    groups = (far, far_other)
    values, base = [], {}
    for chunk in (0, 1):
        for name, now in (("far", groups), ("near", (here, near))):
            base[name, chunk] = len(values)
            values += [count, response_lengths[0]] + [position_of(*g) for g in now]
            values += [column_of(0, 0, chunk)] + pieces_at
    base["place"] = len(values)
    values += [column_of(*g, chunk) for chunk in (0, 1) for g in groups]
    values += [column_of(*near, chunk) for chunk in (0, 1)]
    scalars = jnp.stack(values).astype(jnp.int32)

    q_far_0 = to_other(query_slice(*far, 0), *far)
    q_own = jnp.concatenate([query_slice(0, 0, chunk) for chunk in (0, 1)])
    q_near = to_other(jnp.concatenate([query_slice(*near, chunk) for chunk in (0, 1)]), *near)
    parts_0, q_far_0, w_next, scalars, sum_info, gate = lax.optimization_barrier(
        (parts_0, q_far_0, w_next, scalars, sum_info, gate)
    )
    parts_0 = lax.all_to_all(parts_0, CHIPS, 0, 0, tiled=True)
    parts_1 = project(swap, w_next, image, image_other, 0, w_own)
    parts_1 = project(swap, w_far, image, image_other, 1, parts_1)
    parts_1, parts_0, q_near, q_own = lax.optimization_barrier((parts_1, parts_0, q_near, q_own))
    parts_1 = lax.all_to_all(parts_1, CHIPS, 0, 0, tiled=True)
    sum_0 = sum_parts(sum_info, parts_0)
    kv_0 = [in_hbm(x) for x in [sum_0] + [lax.ppermute(sum_0, Y, ring(4, step)) for step in (1, 3, 2)]]
    q_send, _ = lax.optimization_barrier((query_slice(*far_other, 0), sum_0))
    q_far_other_0 = to_other(q_send, *far_other)

    sum_1 = sum_parts(sum_info, parts_1)
    kv_1 = [sum_1] + [lax.ppermute(sum_1, Y, ring(4, step)) for step in (1, 3, 2)]
    q_send, sum_1 = lax.optimization_barrier(([query_slice(*other, 1) for other in groups], sum_1))
    q_1 = [(to_other(x, *other), 0) for x, other in zip(q_send, groups)]

    q_0 = [(x, 0) for x in (q_far_0, q_far_other_0)]
    gives_0 = attend(scalars, base["far", 0], gate, [(kv_0, q_0)], w_own, head_dim, None, True)
    gives_1 = attend(scalars, base["far", 1], gate, [(kv_1, q_1)], gives_0[0], head_dim, None, True)
    got = [to_other(value, *other) for gives in (gives_0, gives_1) for value, other in zip(gives, groups)]
    out = gives_1[0]
    for chunk, kv in enumerate((kv_0, kv_1)):
        job = (kv, [(q_own, chunk), (q_near, chunk)])
        out, give = attend(scalars, base["near", chunk], gate, [job], out, head_dim, q.shape, True)
        got.append(to_other(give, *near))
    out = place(scalars, base["place"], got, out)
    return out[None]


def solution(mesh):
    fine = Mesh(mesh.devices.reshape(2, 4, 2, 4, 2), (XL, Z, XH, Y, C))
    sample, head = (XL, Z), (XH, Y, C)
    placed = (
        P(sample, head, None),
        P(sample, None, head),
        P(head, sample, None, None),
        P(),
        P(sample),
        P(sample),
    )
    return jax.shard_map(
        on_device, mesh=fine, in_specs=placed, out_specs=P(sample, head, None), check_vma=False
    )
```
